256 devices in a mesh: dp: 4 (over x), context: 64 (over y, z, core).
Axes of the slice: x: 4, y: 4, z: 8, core: 2. Of those that a mesh axis runs over, the one named last changes fastest.
Arguments:
- queries: bfloat16 [32768, 8192], P(('dp', 'context')), parts along dimension 0, may hold values from -6 to 6
- out_grad: bfloat16 [32768, 8192], P(('dp', 'context')), parts along dimension 0, may hold values from -6 to 6
- image_keys: bfloat16 [4096, 1024], P(('dp', 'context')), parts along dimension 0, may hold values from -6 to 6
- image_values: bfloat16 [4096, 1024], P(('dp', 'context')), parts along dimension 0, may hold values from -6 to 6
- link_ids: int32 [16], P('dp'), parts along dimension 0, may hold values from 0 to 3, each once
- token_counts: int32 [16], P('dp'), parts along dimension 0, may hold values from 1 to 256, 640 in all
- tile_mask: int32 [256, 4], P('dp'), parts along dimension 0, may hold values from 0 to 1, as said below
Outputs:
- query_grad: bfloat16 [32768, 8192], P(('dp', 'context')), parts along dimension 0
- key_grad: float32 [4096, 1024], P(('dp', 'context')), parts along dimension 0
- value_grad: float32 [4096, 1024], P(('dp', 'context')), parts along dimension 0
The draws below stay inside these ranges and needn't reach their ends.
There are 4 independent parts, one for each index of `dp`. The reference program is written for one: setup_inputs(seed, part) draws one part's arguments, and reference() takes and returns one part's arrays. A program takes and returns all parts, laid end to end along the dimension named above; each array names one. Nothing has to cross between parts.
Inputs may be any that keep to these rules, and one draw needn't show every extreme that they name: `link_ids`: a permutation of the stored images. `token_counts`: one image has all 256 slots live. tile_mask[t, p] = 1 exactly when t is at or past the start tile of link position p; position 0 starts at tile 0.
All inputs are finite; a program needn't handle non-finite values.
Results may differ from the reference program's by a relative error of at most 0.0066.
Values may be sent and summed in bfloat16 or wider, within the bound.
A program may use at most 192 MiB of HBM per device.

```python
import math
import jax
import jax.numpy as jnp
import numpy as np
from jax import lax

H = 64
KVH = 8
HD = 128
TILE = 128
IMAGES = 4
VIS = 256
TOKENS = 8192
TILES = 64


def draw_queries(key, part):
    key = jax.random.fold_in(key, 11)
    return jnp.clip(jax.random.normal(key, (TOKENS, H * HD), jnp.float32), -6.0, 6.0).astype(jnp.bfloat16)


def draw_image_keys(key, part):
    key = jax.random.fold_in(key, 12)
    return jnp.clip(jax.random.normal(key, (IMAGES * VIS, KVH * HD), jnp.float32), -6.0, 6.0).astype(jnp.bfloat16)


def draw_tile_mask(key, part):
    key = jax.random.fold_in(key, 13)
    starts = jax.random.randint(key, (IMAGES,), 1, TILES, dtype=jnp.int32)
    starts = jnp.where(jnp.arange(IMAGES, dtype=jnp.int32) == 0, 0, starts)
    tiles = jnp.arange(TILES, dtype=jnp.int32)[:, None]
    return (tiles >= starts[None, :]).astype(jnp.int32)


def shard_levels(stream_key, dims, split, smallest, largest):
    factor_of, own = 1.0, jax.random.fold_in(stream_key, 6)
    for dim, blocks in split:
        heights = jnp.exp(jax.random.uniform(jax.random.fold_in(own, dim), (blocks,), jnp.float32, smallest / len(split), largest / len(split)))
        factor_of = factor_of * jnp.repeat(heights, dims[dim] // blocks).reshape([-1 if axis == dim else 1 for axis in range(len(dims))])
    return factor_of


def profile(number_of, total, most, skew):
    weights = [(1 << 20) // math.isqrt(rank ** skew) + 1 for rank in range(2, number_of + 1)]
    spare, counts = total - most - (number_of - 1), [1] * (number_of - 1)
    while spare > 0:
        candidates = [i for i in range(number_of - 1) if counts[i] < most]
        mass, left = sum([weights[i] for i in candidates]), spare
        for i in candidates:
            addition = min(most - counts[i], max(1, left * weights[i] // mass), spare)
            counts[i] = counts[i] + addition
            spare = spare - addition
    return np.array([most] + counts)


def uneven(stream_key, number_of, total, limit, slope):
    if number_of == 2:
        one = jax.random.randint(stream_key, (), max(1, total - limit), min(limit, total - 1) + 1)
        return jnp.stack([one, total - one])
    tallies = jnp.asarray(profile(number_of, total, limit, slope), jnp.int32)
    couples = (number_of - 1) // 2
    giver, sink = tallies[1:1 + 2 * couples:2], tallies[2:2 + 2 * couples:2]
    margin = jnp.minimum(giver - 1, limit - sink)
    passed = jax.random.randint(jax.random.fold_in(stream_key, 1), (couples,), 0, 1 << 20) % (margin + 1)
    tallies = tallies.at[1:1 + 2 * couples:2].set(giver - passed).at[2:2 + 2 * couples:2].set(sink + passed)
    return tallies[jax.random.permutation(jax.random.fold_in(stream_key, 2), number_of)]


def gaussian(stream_key, extent, scale, limit, shards=(), kind=jnp.bfloat16):
    values = jax.random.normal(stream_key, extent, jnp.float32) * scale
    if len(shards) > 0:
        values = shard_levels(stream_key, extent, shards, -0.22, 0.18) * values
    return jnp.clip(values, min=-limit, max=limit).astype(kind)


def setup_inputs(seed: int = 0, part: int = 0) -> dict:
    arg_keys = jax.random.split(jax.random.key(seed), 8)
    part_keys = jax.random.split(jax.random.fold_in(arg_keys[7], part), 8)
    queries = draw_queries(jax.random.fold_in(jax.random.fold_in(arg_keys[7], part), 71), part)
    out_grad = gaussian(part_keys[1], (TOKENS, H * HD), 1.0, 6.0, ((0, 64),))
    image_keys = draw_image_keys(jax.random.fold_in(jax.random.fold_in(arg_keys[7], part), 71), part)
    image_values = gaussian(part_keys[3], (IMAGES * VIS, KVH * HD), 1.0, 6.0, ((0, 64),))
    link_ids = jax.random.permutation(part_keys[4], IMAGES).astype(jnp.int32)
    token_counts = uneven(part_keys[5], IMAGES, 5 * VIS // 2, VIS, 2).astype(jnp.int32)
    tile_mask = draw_tile_mask(jax.random.fold_in(jax.random.fold_in(arg_keys[7], part), 71), part)
    return {"queries": queries, "out_grad": out_grad, "image_keys": image_keys, "image_values": image_values, "link_ids": link_ids, "token_counts": token_counts, "tile_mask": tile_mask}


def link_table(link_ids, tile_mask):
    onehot = (link_ids[:, None] == jnp.arange(IMAGES, dtype=jnp.int32)[None, :]).astype(jnp.float32)
    return lax.optimization_barrier(jnp.sum(tile_mask.astype(jnp.float32)[:, :, None] * onehot[None, :, :], axis=1))

def key_valid(token_counts):
    slots = jnp.arange(IMAGES * VIS, dtype=jnp.int32)
    owner = slots // VIS
    inside = slots - owner * VIS
    same = owner[None, :] == jnp.arange(IMAGES, dtype=jnp.int32)[:, None]
    live = inside[None, :] < token_counts[:, None]
    return (same & live).astype(jnp.float32)

def allowed_block(table, valid, row_start, rows):
    tiles = lax.dynamic_slice_in_dim(table, (row_start // TILE).astype(jnp.int32), rows // TILE, 0)
    spread = jnp.repeat(tiles, TILE, axis=0)
    allowed = spread[:, 0:1] * valid[0][None, :]
    for image in range(1, IMAGES):
        allowed = allowed + spread[:, image:image + 1] * valid[image][None, :]
    return allowed

def group_backward(query_rows, grad_rows, key_head, value_head, allowed):
    score_scale = 1.0 / math.sqrt(HD)
    q32 = query_rows.astype(jnp.float32)
    g32 = grad_rows.astype(jnp.float32)
    k32 = key_head.astype(jnp.float32)
    v32 = value_head.astype(jnp.float32)
    scores = jnp.einsum('rgd,ld->grl', q32, k32) * score_scale
    scores = jnp.where(allowed[None] > 0, scores, jnp.float32(-1e+30))
    row_max = lax.optimization_barrier(jnp.max(scores, axis=-1, keepdims=True))
    weights = jnp.exp(scores - row_max)
    probs = weights / lax.optimization_barrier(jnp.sum(weights, axis=-1, keepdims=True))
    probs_low = probs.astype(jnp.bfloat16)
    dprobs = jnp.einsum('rgd,ld->grl', g32, v32)
    row_delta = lax.optimization_barrier(jnp.sum(probs * dprobs, axis=-1, keepdims=True))
    dscores = (probs * (dprobs - row_delta) * score_scale).astype(jnp.bfloat16).astype(jnp.float32)
    query_part = jnp.einsum('grl,ld->rgd', dscores, k32)
    key_part = jnp.einsum('grl,rgd->ld', dscores, q32)
    value_part = jnp.einsum('grl,rgd->ld', probs_low.astype(jnp.float32), g32)
    return (query_part, key_part, value_part)

def reference(queries, out_grad, image_keys, image_values, link_ids, token_counts, tile_mask):
    table = link_table(link_ids, tile_mask)
    valid = key_valid(token_counts)
    rows_total = queries.shape[0]
    block = math.gcd(rows_total, 512)
    group_size = H // KVH
    slots = image_keys.shape[0]

    def step(carry, start_block):
        key_acc, value_acc = carry
        row_start = start_block * block
        q_rows = lax.dynamic_slice_in_dim(queries, row_start, block, 0)
        g_rows = lax.dynamic_slice_in_dim(out_grad, row_start, block, 0)
        allowed = allowed_block(table, valid, row_start, block)
        query_parts, key_parts, value_parts = ([], [], [])
        for group in range(KVH):
            lo_col = group * group_size * HD
            hi_col = (group + 1) * group_size * HD
            q_blk = q_rows[:, lo_col:hi_col].reshape(block, group_size, HD)
            g_blk = g_rows[:, lo_col:hi_col].reshape(block, group_size, HD)
            key_head = image_keys[:, group * HD:(group + 1) * HD]
            value_head = image_values[:, group * HD:(group + 1) * HD]
            query_part, key_part, value_part = group_backward(q_blk, g_blk, key_head, value_head, allowed)
            query_parts.append(query_part.reshape(block, group_size * HD))
            key_parts.append(key_part)
            value_parts.append(value_part)
        new_carry = (key_acc + jnp.concatenate(key_parts, axis=1), value_acc + jnp.concatenate(value_parts, axis=1))
        return (new_carry, jnp.concatenate(query_parts, axis=1).astype(jnp.bfloat16))
    start = (jnp.zeros((slots, KVH * HD), jnp.float32), jnp.zeros((slots, KVH * HD), jnp.float32))
    (key_grad, value_grad), blocks = lax.scan(step, start, jnp.arange(rows_total // block, dtype=jnp.int32))
    query_grad = blocks.reshape(rows_total, H * HD)
    return (query_grad, key_grad, value_grad)
```

```python
import functools
import math

import jax
import jax.numpy as jnp
from jax import lax
from jax.experimental import pallas as pl
from jax.experimental.pallas import tpu as pltpu
from jax.sharding import PartitionSpec as P

H = 64
KVH = 8
HD = 128
TILE = 128
IMAGES = 4
VIS = 256
GROUP = H // KVH
PAIRS = GROUP // 2
NY = 4
NZ = 8
ROWS = 16
BLOCKS = IMAGES * VIS // ROWS
LIVE = 42
L = LIVE * ROWS
CHUNK = 112
SCALE = 1.0 / math.sqrt(HD)
SCALE2 = SCALE * math.log2(math.e)
NEG = -1e30
Z_GROUPS = ((0, 1), (1, 3), (4, 4))
MESH = pl.DeviceIdType.MESH
f32 = jnp.float32
bf16 = jnp.bfloat16


def dot(a, b, ca, cb):
    return lax.dot_general(a, b, (((ca,), (cb,)), ((), ())), preferred_element_type=f32)


def device(y, z, k):
    return {"context": (y * NZ + z) * 2 + k}


def remote(src, dst, sems, at, target):
    send, recv = sems
    return pltpu.make_async_remote_copy(
        src_ref=src,
        dst_ref=dst,
        send_sem=send.at[at],
        recv_sem=recv.at[at],
        device_id=target,
        device_id_type=MESH,
    )


def kernel(
    links, counts, tiles, q_hbm, g_hbm, k_in, v_in,
    dq_hbm, dk_out, dv_out,
    q, g, dq, kv, cur, kaug, vc, kt, s0, s1, d0, d1, e_buf, p0, p1, w0, w1, dk_acc, dv_acc,
    rs_full, rs_sib, rs_y, rs_yr, rs_z, rs_zr, src_tbl, dst_tbl, row_tbl,
    load_sem, dq_sem, zs, zr, ys, yr, cs, cr, rcs, rcr, rys, ryr, rzs, rzr,
):
    c = lax.axis_index("context")
    y, z, k = c // (2 * NZ), lax.rem(c // 2, NZ), lax.rem(c, 2)
    other = 1 - k
    yy = [lax.rem(y + d, NY) for d in range(NY)]
    zz = [lax.rem(z + d, NZ) for d in range(NZ)]
    sibling = device(y, z, other)
    y_peer = [device(yy[d], z, k) for d in range(NY)]
    z_peer = [device(y, zz[d], k) for d in range(NZ)]
    z_sem, y_sem, c_sem = (zs, zr), (ys, yr), (cs, cr)
    rc_sem, ry_sem, rz_sem = (rcs, rcr), (rys, ryr), (rzs, rzr)

    q_load = pltpu.make_async_copy(q_hbm, q, load_sem.at[0])
    g_load = pltpu.make_async_copy(g_hbm, g, load_sem.at[1])
    q_load.start()
    g_load.start()

    barrier = pltpu.get_barrier_semaphore()
    peers = [sibling] + y_peer[1:] + z_peer[1:]
    for peer in peers:
        pl.semaphore_signal(barrier, inc=1, device_id=peer, device_id_type=MESH)
    for h in range(KVH):
        kv[h, k, y, z, 0] = k_in[:, h * HD : (h + 1) * HD]
        kv[h, k, y, z, 1] = v_in[:, h * HD : (h + 1) * HD]
    pl.semaphore_wait(barrier, len(peers))

    def z_send(group, d):
        heads = pl.ds(*Z_GROUPS[group])
        mine = kv.at[heads, k, y, z]
        return remote(mine, mine, z_sem, (group, d - 1), z_peer[d])

    def z_recv(group, d):
        heads = pl.ds(*Z_GROUPS[group])
        return remote(kv.at[heads, k, y, z], kv.at[heads, k, y, zz[NZ - d]], z_sem, (group, d - 1), z_peer[d])

    def y_send(h, d):
        return remote(kv.at[h, k, y], kv.at[h, k, y], y_sem, (h, d - 1), y_peer[d])

    def y_recv(h, d):
        return remote(kv.at[h, k, y], kv.at[h, k, yy[NY - d]], y_sem, (h, d - 1), y_peer[d])

    def c_send(h):
        return remote(kv.at[h, k], kv.at[h, k], c_sem, (h,), sibling)

    def c_recv(h):
        return remote(kv.at[h, k], kv.at[h, other], c_sem, (h,), sibling)

    for group in range(len(Z_GROUPS)):
        for d in range(1, NZ):
            z_send(group, d).start()

    def pass_on(group):
        for d in range(1, NZ):
            z_recv(group, d).wait_recv()
        first, number = Z_GROUPS[group]
        for h in range(first, first + number):
            for d in range(1, NY):
                y_send(h, d).start()

    pass_on(0)

    zero = jnp.int32(0)
    live_rows, first_block = [], [zero]
    for image in range(IMAGES):
        seen = zero
        for p in range(IMAGES):
            seen = seen + jnp.where(links[p] == image, tiles[c, p], 0)
        live_rows.append(jnp.where(seen > 0, counts[image], 0))
        first_block.append(first_block[-1] + (live_rows[-1] + (ROWS - 1)) // ROWS)
    spare = first_block[IMAGES]

    def fill_src(b, _):
        image, base, rows = zero, zero, live_rows[0]
        for i in range(1, IMAGES):
            past = b >= first_block[i]
            image = jnp.where(past, i, image)
            base = jnp.where(past, first_block[i], base)
            rows = jnp.where(past, live_rows[i], rows)
        u = jnp.minimum(b - base, VIS // ROWS - 1)
        src_tbl[b] = lax.rem(u, 2) * (NY * NZ) + image * NZ + u // 2
        row_tbl[b] = jnp.where(b < spare, rows - (b - base) * ROWS, 0)
        return 0

    lax.fori_loop(0, LIVE, fill_src, 0)
    for image in range(IMAGES):

        def fill_dst(u, _):
            at = lax.rem(u, 2) * (NY * NZ) + image * NZ + u // 2
            dst_tbl[at] = jnp.where(u * ROWS < live_rows[image], first_block[image] + u, LIVE)
            return 0

        lax.fori_loop(0, VIS // ROWS, fill_dst, 0)

    lane = lax.broadcasted_iota(jnp.int32, (ROWS, HD), 1)
    row = lax.broadcasted_iota(jnp.int32, (ROWS, HD), 0)

    def fill_bias(b, _):
        dead = jnp.logical_and(lane == 0, row >= row_tbl[b])
        kaug[b, :, HD:] = jnp.where(dead, NEG, 0.0).astype(bf16)
        return 0

    lax.fori_loop(0, LIVE, fill_bias, 0)
    dk_acc[LIVE] = jnp.zeros((ROWS, HD), f32)
    dv_acc[LIVE] = jnp.zeros((ROWS, HD), f32)

    def compact(h):
        flat = 2 * NY * NZ
        cur[...] = kv[h].reshape(flat, 2, ROWS, HD)
        for b in range(LIVE):
            kaug[b, :, :HD] = cur[src_tbl[b], 0]
            vc[b] = cur[src_tbl[b], 1]

    def transpose_keys():
        kt[...] = kaug[...].reshape(L, 2 * HD)[:, :HD].T

    s_buf, d_buf, p_buf, w_buf = (s0, s1), (d0, d1), (p0, p1), (w0, w1)
    ones = jnp.where(lax.broadcasted_iota(jnp.int32, (2 * TILE, HD), 1) == 0, 1.0, 0.0).astype(bf16)

    def two_heads(ref, h, pair):
        start = pl.multiple_of(h * (GROUP * HD) + pair * (2 * HD), 2 * HD)
        both = ref[:, pl.ds(start, 2 * HD)]
        return jnp.concatenate([both[:, :HD], both[:, HD:]], axis=0)

    def front(h, pair, slot):
        rows_q = jnp.concatenate([two_heads(q, h, pair), ones], axis=1)
        s_buf[slot][...] = dot(kaug[...].reshape(L, 2 * HD), rows_q, 1, 1)
        d_buf[slot][...] = dot(vc[...].reshape(L, HD), two_heads(g, h, pair), 1, 1)

    def middle(slot):
        tops, sums, deltas = [], [], []
        lanes = 2 * TILE
        for i in range(L // CHUNK):
            at = slice(i * CHUNK, (i + 1) * CHUNK)
            s = s_buf[slot][at, :]
            top = jnp.max(s, axis=0, keepdims=True) * SCALE2
            e = jnp.exp2(s * SCALE2 - top)
            e_buf[at, :] = e
            sums.append(jnp.sum(e.reshape(CHUNK // 8, 8, lanes), axis=0))
            deltas.append(jnp.sum((e * d_buf[slot][at, :]).reshape(CHUNK // 8, 8, lanes), axis=0))
            tops.append(top)
        top = functools.reduce(jnp.maximum, tops)
        weight = [jnp.exp2(t - top) for t in tops]
        total = jnp.sum(sum(a * b for a, b in zip(sums, weight)), axis=0, keepdims=True)
        delta = jnp.sum(sum(a * b for a, b in zip(deltas, weight)), axis=0, keepdims=True)
        inverse = 1.0 / total
        delta = delta * inverse
        for i in range(L // CHUNK):
            at = slice(i * CHUNK, (i + 1) * CHUNK)
            prob = e_buf[at, :] * (weight[i] * inverse)
            p_buf[slot][at, :] = prob.astype(bf16)
            w_buf[slot][at, :] = (prob * (d_buf[slot][at, :] - delta)).astype(bf16)

    def back(h, pair, slot, first):
        dqt = dot(kt[...], w_buf[slot][...], 1, 0) * SCALE
        for j in range(2):
            start = pl.multiple_of(h * (GROUP * HD) + pair * (2 * HD) + j * HD, HD)
            dq[:, pl.ds(start, HD)] = dqt[:, j * TILE : (j + 1) * TILE].T.astype(bf16)
        dv = dot(p_buf[slot][...], two_heads(g, h, pair), 1, 0).reshape(LIVE, ROWS, HD)
        dk = dot(w_buf[slot][...], two_heads(q, h, pair), 1, 0).reshape(LIVE, ROWS, HD)
        if first:
            dv_acc[:LIVE] = dv
            dk_acc[:LIVE] = dk
        else:
            dv_acc[:LIVE] += dv
            dk_acc[:LIVE] += dk

    def rc_send(h):
        return remote(rs_full.at[h, other], rs_sib.at[h], rc_sem, (h,), sibling)

    def ry_send(h, d):
        return remote(rs_y.at[h, yy[d]], rs_yr.at[h, d - 1], ry_sem, (h, d - 1), y_peer[d])

    def rz_send(h, d):
        return remote(rs_z.at[h, zz[d]], rs_zr.at[h, d - 1], rz_sem, (h, d - 1), z_peer[d])

    def dq_store(h):
        cols = pl.ds(pl.multiple_of(h * (GROUP * HD), GROUP * HD), GROUP * HD)
        return pltpu.make_async_copy(dq.at[:, cols], dq_hbm.at[:, cols], dq_sem.at[h])

    def finish(h):
        for plane in range(2):
            for a in range(NY):
                for b in range(NZ):
                    at = dst_tbl[plane * (NY * NZ) + a * NZ + b]
                    rs_full[h, plane, a, b, 0] = (dk_acc[at] * SCALE).astype(bf16)
                    rs_full[h, plane, a, b, 1] = dv_acc[at].astype(bf16)
        rc_send(h).start()
        dq_store(h).start()

    def reduce_core(h):
        rc_send(h).wait_recv()
        for a in range(NY):
            rs_y[h, a] = (rs_full[h, k, a].astype(f32) + rs_sib[h, a].astype(f32)).astype(bf16)
        for d in range(1, NY):
            ry_send(h, d).start()

    def reduce_y(h):
        total = rs_y[h, y].astype(f32)
        for d in range(1, NY):
            ry_send(h, d).wait_recv()
            total = total + rs_yr[h, d - 1].astype(f32)
        rs_z[h] = total.astype(bf16)
        for d in range(1, NZ):
            rz_send(h, d).start()

    def reduce_z(h):
        total = rs_z[h, z].astype(f32)
        for d in range(1, NZ):
            rz_send(h, d).wait_recv()
            total = total + rs_zr[h, d - 1].astype(f32)
        cols = pl.ds(pl.multiple_of(h * HD, HD), HD)
        dk_out[:, cols] = total[0]
        dv_out[:, cols] = total[1]

    def bring(h):
        for d in range(1, NY):
            y_recv(h, d).wait_recv()
        c_send(h).start()

    bring(0)
    pass_on(1)
    c_recv(0).wait_recv()
    compact(0)
    q_load.wait()
    g_load.wait()
    front(0, 0, 0)

    def step(h, _):
        front(h, 1, 1)
        middle(0)

        @pl.when(h == 0)
        def _():
            pass_on(2)

        @pl.when(h > 0)
        def _():
            back(h - 1, 3, 1, False)
            finish(h - 1)

        @pl.when(h < KVH - 1)
        def _():
            bring(h + 1)

        transpose_keys()
        front(h, 2, 0)
        middle(1)
        back(h, 0, 0, True)

        @pl.when(h >= 1)
        def _():
            reduce_core(h - 1)

        front(h, 3, 1)
        middle(0)
        back(h, 1, 1, False)

        @pl.when(h >= 3)
        def _():
            reduce_y(h - 3)

        @pl.when(h >= 5)
        def _():
            reduce_z(h - 5)

        @pl.when(h < KVH - 1)
        def _():
            c_recv(h + 1).wait_recv()
            compact(h + 1)

        front(jnp.minimum(h + 1, KVH - 1), 0, 0)
        middle(1)
        back(h, 2, 0, False)
        return 0

    lax.fori_loop(0, KVH, step, 0)
    back(KVH - 1, 3, 1, False)
    finish(KVH - 1)
    reduce_y(KVH - 3)
    reduce_z(KVH - 5)
    reduce_core(KVH - 1)
    reduce_y(KVH - 2)
    reduce_z(KVH - 4)
    reduce_y(KVH - 1)
    reduce_z(KVH - 3)
    reduce_z(KVH - 2)
    reduce_z(KVH - 1)

    for group in range(len(Z_GROUPS)):
        for d in range(1, NZ):
            z_send(group, d).wait_send()

    def drain(h, _):
        for d in range(1, NY):
            y_send(h, d).wait_send()
            ry_send(h, d).wait_send()
        for d in range(1, NZ):
            rz_send(h, d).wait_send()
        c_send(h).wait_send()
        rc_send(h).wait_send()
        dq_store(h).wait()
        return 0

    lax.fori_loop(0, KVH, drain, 0)


def body(queries, out_grad, image_keys, image_values, link_ids, token_counts, tile_mask):
    smem = pl.BlockSpec(memory_space=pltpu.SMEM)
    vmem = pl.BlockSpec(memory_space=pltpu.VMEM)
    hbm = pl.BlockSpec(memory_space=pl.ANY)
    dma = pltpu.SemaphoreType.DMA
    lanes = 2 * TILE
    scratch = [
        pltpu.VMEM((TILE, H * HD), bf16),
        pltpu.VMEM((TILE, H * HD), bf16),
        pltpu.VMEM((TILE, H * HD), bf16),
        pltpu.VMEM((KVH, 2, NY, NZ, 2, ROWS, HD), bf16),
        pltpu.VMEM((BLOCKS, 2, ROWS, HD), bf16),
        pltpu.VMEM((LIVE, ROWS, 2 * HD), bf16),
        pltpu.VMEM((LIVE, ROWS, HD), bf16),
        pltpu.VMEM((HD, L), bf16),
        pltpu.VMEM((L, lanes), f32),
        pltpu.VMEM((L, lanes), f32),
        pltpu.VMEM((L, lanes), f32),
        pltpu.VMEM((L, lanes), f32),
        pltpu.VMEM((L, lanes), f32),
        pltpu.VMEM((L, lanes), bf16),
        pltpu.VMEM((L, lanes), bf16),
        pltpu.VMEM((L, lanes), bf16),
        pltpu.VMEM((L, lanes), bf16),
        pltpu.VMEM((LIVE + 1, ROWS, HD), f32),
        pltpu.VMEM((LIVE + 1, ROWS, HD), f32),
        pltpu.VMEM((KVH, 2, NY, NZ, 2, ROWS, HD), bf16),
        pltpu.VMEM((KVH, NY, NZ, 2, ROWS, HD), bf16),
        pltpu.VMEM((KVH, NY, NZ, 2, ROWS, HD), bf16),
        pltpu.VMEM((KVH, NY - 1, NZ, 2, ROWS, HD), bf16),
        pltpu.VMEM((KVH, NZ, 2, ROWS, HD), bf16),
        pltpu.VMEM((KVH, NZ - 1, 2, ROWS, HD), bf16),
        pltpu.SMEM((LIVE,), jnp.int32),
        pltpu.SMEM((BLOCKS,), jnp.int32),
        pltpu.SMEM((LIVE,), jnp.int32),
        dma((2,)),
        dma((KVH,)),
        dma((len(Z_GROUPS), NZ - 1)),
        dma((len(Z_GROUPS), NZ - 1)),
        dma((KVH, NY - 1)),
        dma((KVH, NY - 1)),
        dma((KVH,)),
        dma((KVH,)),
        dma((KVH,)),
        dma((KVH,)),
        dma((KVH, NY - 1)),
        dma((KVH, NY - 1)),
        dma((KVH, NZ - 1)),
        dma((KVH, NZ - 1)),
    ]
    return pl.pallas_call(
        kernel,
        out_shape=(
            jax.ShapeDtypeStruct((TILE, H * HD), bf16),
            jax.ShapeDtypeStruct((ROWS, KVH * HD), f32),
            jax.ShapeDtypeStruct((ROWS, KVH * HD), f32),
        ),
        in_specs=[smem, smem, smem, hbm, hbm, vmem, vmem],
        out_specs=[hbm, vmem, vmem],
        scratch_shapes=scratch,
        compiler_params=pltpu.CompilerParams(
            collective_id=0, has_side_effects=True, vmem_limit_bytes=56 << 20
        ),
        cost_estimate=pl.CostEstimate(
            flops=5 * 2 * TILE * H * L * HD, bytes_accessed=8 << 20, transcendentals=TILE * H * L
        ),
    )(link_ids, token_counts, tile_mask, queries, out_grad, image_keys, image_values)


def solution(mesh):
    rows = P(("dp", "context"), None)
    return jax.shard_map(
        body,
        mesh=mesh,
        in_specs=(rows, rows, rows, rows, P("dp"), P("dp"), P("dp", None)),
        out_specs=(rows, rows, rows),
        check_vma=False,
    )
```

```python
import functools
import math

import jax
import jax.numpy as jnp
from jax import lax
from jax.experimental import pallas as pl
from jax.experimental.pallas import tpu as pltpu
from jax.sharding import PartitionSpec as P

H = 64
KVH = 8
HD = 128
TILE = 128
IMAGES = 4
VIS = 256
GROUP = H // KVH
PAIRS = GROUP // 2
NY = 4
NZ = 8
ROWS = 16
BLOCKS = IMAGES * VIS // ROWS
LIVE = 42
L = LIVE * ROWS
CHUNK = 112
SCALE = 1.0 / math.sqrt(HD)
SCALE2 = SCALE * math.log2(math.e)
NEG = -1e30
HAND_STEPS = 4
Z_FIRST = 5
AHEAD = 4
SPARE = KVH
MESH = pl.DeviceIdType.MESH
f32 = jnp.float32
bf16 = jnp.bfloat16


def dot(a, b, ca, cb):
    return lax.dot_general(a, b, (((ca,), (cb,)), ((), ())), preferred_element_type=f32)


def device(y, z, k):
    return {"context": (y * NZ + z) * 2 + k}


def remote(src, dst, sems, at, target):
    send, recv = sems
    return pltpu.make_async_remote_copy(
        src_ref=src,
        dst_ref=dst,
        send_sem=send.at[at],
        recv_sem=recv.at[at],
        device_id=target,
        device_id_type=MESH,
    )


def kernel(
    links, counts, tiles, q_hbm, g_hbm, k_in, v_in,
    dq_hbm, dk_out, dv_out,
    q, g, dq, kv, cur, kaug, vc, kt, s0, s1, d0, d1, e_buf, p0, p1, w0, w1, dk_acc, dv_acc,
    rs_full, rs_sib, rs_y, rs_yr, rs_z, rs_zr, sums, src_tbl, dst_tbl, row_tbl,
    load_sem, dq_sem, zs, zr, ys, yr, cs, cr, rcs, rcr, rys, ryr, rzs, rzr,
):
    c = lax.axis_index("context")
    y, z, k = c // (2 * NZ), lax.rem(c // 2, NZ), lax.rem(c, 2)
    other = 1 - k
    yy = [lax.rem(y + d, NY) for d in range(NY)]
    zz = [lax.rem(z + d, NZ) for d in range(NZ)]
    sibling = device(y, z, other)
    y_peer = [device(yy[d], z, k) for d in range(NY)]
    z_peer = [device(y, zz[d], k) for d in range(NZ)]
    z_sem, y_sem, c_sem = (zs, zr), (ys, yr), (cs, cr)
    rc_sem, ry_sem, rz_sem = (rcs, rcr), (rys, ryr), (rzs, rzr)

    q_load = pltpu.make_async_copy(q_hbm, q, load_sem.at[0])
    g_load = pltpu.make_async_copy(g_hbm, g, load_sem.at[1])
    q_load.start()
    g_load.start()

    barrier = pltpu.get_barrier_semaphore()
    peers = [sibling] + y_peer[1:] + z_peer[1:]
    for peer in peers:
        pl.semaphore_signal(barrier, inc=1, device_id=peer, device_id_type=MESH)
    for h in range(KVH):
        kv[h, k, y, z, 0] = k_in[:, h * HD : (h + 1) * HD]
        kv[h, k, y, z, 1] = v_in[:, h * HD : (h + 1) * HD]
    pl.semaphore_wait(barrier, len(peers))

    def z_send(h, d):
        return remote(kv.at[h, k, y, z], kv.at[h, k, y, z], z_sem, (h, d - 1), z_peer[d])

    def z_recv(h, d):
        return remote(kv.at[h, k, y, z], kv.at[h, k, y, zz[NZ - d]], z_sem, (h, d - 1), z_peer[d])

    def y_send(h, d):
        return remote(kv.at[h, k, y], kv.at[h, k, y], y_sem, (h, d - 1), y_peer[d])

    def y_recv(h, d):
        return remote(kv.at[h, k, y], kv.at[h, k, yy[NY - d]], y_sem, (h, d - 1), y_peer[d])

    def c_send(h):
        return remote(kv.at[h, k], kv.at[h, k], c_sem, (h,), sibling)

    def c_recv(h):
        return remote(kv.at[h, k], kv.at[h, other], c_sem, (h,), sibling)

    def block_send(h, d):
        return remote(kv.at[h, k, y, z], kv.at[h, k, y, z], y_sem, (h, d - 1), y_peer[d])

    def block_recv(h, d):
        return remote(kv.at[h, k, y, z], kv.at[h, k, yy[NY - d], z], y_sem, (h, d - 1), y_peer[d])

    def column_send(h, d):
        return remote(kv.at[h, k, :, z], kv.at[h, k, :, z], z_sem, (h, d - 1), z_peer[d])

    def column_recv(h, d):
        return remote(kv.at[h, k, :, z], kv.at[h, k, :, zz[NZ - d]], z_sem, (h, d - 1), z_peer[d])

    def start_column(h):
        for d in range(1, NY):
            block_recv(h, d).wait_recv()
        for d in range(1, NZ):
            column_send(h, d).start()

    def start_y(h):
        for d in range(1, NZ):
            z_recv(h, d).wait_recv()
        for d in range(1, NY):
            y_send(h, d).start()

    def start_c(h):
        for d in range(1, NY):
            y_recv(h, d).wait_recv()
        c_send(h).start()

    def start_c_late(h):
        for d in range(1, NZ):
            column_recv(h, d).wait_recv()
        c_send(h).start()

    for h in range(KVH):
        if h < Z_FIRST:
            for d in range(1, NZ):
                z_send(h, d).start()
        else:
            for d in range(1, NY):
                block_send(h, d).start()

    def prepare():
        zero = jnp.int32(0)
        live_rows, first_block = [], [zero]
        for image in range(IMAGES):
            seen = zero
            for p in range(IMAGES):
                seen = seen + jnp.where(links[p] == image, tiles[p, c], 0)
            live_rows.append(jnp.where(seen > 0, counts[image], 0))
            first_block.append(first_block[-1] + (live_rows[-1] + (ROWS - 1)) // ROWS)
        spare = first_block[IMAGES]

        def fill_src(b, _):
            image, base, rows = zero, zero, live_rows[0]
            for i in range(1, IMAGES):
                past = b >= first_block[i]
                image = jnp.where(past, i, image)
                base = jnp.where(past, first_block[i], base)
                rows = jnp.where(past, live_rows[i], rows)
            u = jnp.minimum(b - base, VIS // ROWS - 1)
            src_tbl[b] = lax.rem(u, 2) * (NY * NZ) + image * NZ + u // 2
            row_tbl[b] = jnp.where(b < spare, rows - (b - base) * ROWS, 0)
            return 0

        lax.fori_loop(0, LIVE, fill_src, 0)
        for image in range(IMAGES):

            def fill_dst(u, _):
                at = lax.rem(u, 2) * (NY * NZ) + image * NZ + u // 2
                dst_tbl[at] = jnp.where(u * ROWS < live_rows[image], first_block[image] + u, LIVE)
                return 0

            lax.fori_loop(0, VIS // ROWS, fill_dst, 0)

        lane = lax.broadcasted_iota(jnp.int32, (ROWS, HD), 1)
        row = lax.broadcasted_iota(jnp.int32, (ROWS, HD), 0)

        def fill_bias(b, _):
            dead = jnp.logical_and(lane == 0, row >= row_tbl[b])
            kaug[b, :, HD:] = jnp.where(dead, NEG, 0.0).astype(bf16)
            return 0

        lax.fori_loop(0, LIVE, fill_bias, 0)
        dk_acc[LIVE] = jnp.zeros((ROWS, HD), f32)
        dv_acc[LIVE] = jnp.zeros((ROWS, HD), f32)

    def compact(h):
        flat = 2 * NY * NZ
        cur[...] = kv[h].reshape(flat, 2, ROWS, HD)
        for b in range(LIVE):
            kaug[b, :, :HD] = cur[src_tbl[b], 0]
            vc[b] = cur[src_tbl[b], 1]

    def transpose_keys():
        kt[...] = kaug[...].reshape(L, 2 * HD)[:, :HD].T

    s_buf, d_buf, p_buf, w_buf = (s0, s1), (d0, d1), (p0, p1), (w0, w1)
    ones = jnp.where(lax.broadcasted_iota(jnp.int32, (2 * TILE, HD), 1) == 0, 1.0, 0.0).astype(bf16)

    def two_heads(ref, h, pair):
        start = pl.multiple_of(h * (GROUP * HD) + pair * (2 * HD), 2 * HD)
        both = ref[:, pl.ds(start, 2 * HD)]
        return jnp.concatenate([both[:, :HD], both[:, HD:]], axis=0)

    def front(h, pair, slot):
        rows_q = jnp.concatenate([two_heads(q, h, pair), ones], axis=1)
        s_buf[slot][...] = dot(kaug[...].reshape(L, 2 * HD), rows_q, 1, 1)
        d_buf[slot][...] = dot(vc[...].reshape(L, HD), two_heads(g, h, pair), 1, 1)

    def middle(slot):
        tops, sums, deltas = [], [], []
        lanes = 2 * TILE
        for i in range(L // CHUNK):
            at = slice(i * CHUNK, (i + 1) * CHUNK)
            s = s_buf[slot][at, :]
            top = jnp.max(s, axis=0, keepdims=True) * SCALE2
            e = jnp.exp2(s * SCALE2 - top)
            e_buf[at, :] = e
            sums.append(jnp.sum(e.reshape(CHUNK // 8, 8, lanes), axis=0))
            deltas.append(jnp.sum((e * d_buf[slot][at, :]).reshape(CHUNK // 8, 8, lanes), axis=0))
            tops.append(top)
        top = functools.reduce(jnp.maximum, tops)
        weight = [jnp.exp2(t - top) for t in tops]
        total = jnp.sum(sum(a * b for a, b in zip(sums, weight)), axis=0, keepdims=True)
        delta = jnp.sum(sum(a * b for a, b in zip(deltas, weight)), axis=0, keepdims=True)
        inverse = 1.0 / total
        delta = delta * inverse
        for i in range(L // CHUNK):
            at = slice(i * CHUNK, (i + 1) * CHUNK)
            prob = e_buf[at, :] * (weight[i] * inverse)
            p_buf[slot][at, :] = prob.astype(bf16)
            w_buf[slot][at, :] = (prob * (d_buf[slot][at, :] - delta)).astype(bf16)

    def back(h, pair, slot, first):
        dqt = dot(kt[...], w_buf[slot][...], 1, 0) * SCALE
        for j in range(2):
            start = pl.multiple_of(h * (GROUP * HD) + pair * (2 * HD) + j * HD, HD)
            dq[:, pl.ds(start, HD)] = dqt[:, j * TILE : (j + 1) * TILE].T.astype(bf16)
        dv = dot(p_buf[slot][...], two_heads(g, h, pair), 1, 0).reshape(LIVE, ROWS, HD)
        dk = dot(w_buf[slot][...], two_heads(q, h, pair), 1, 0).reshape(LIVE, ROWS, HD)
        if first:
            dv_acc[:LIVE] = dv
            dk_acc[:LIVE] = dk
        else:
            dv_acc[:LIVE] += dv
            dk_acc[:LIVE] += dk

    def rc_send(h):
        return remote(rs_full.at[h, other], rs_sib.at[h], rc_sem, (h,), sibling)

    def ry_send(h, d):
        return remote(rs_y.at[h, yy[d]], rs_yr.at[h, d - 1], ry_sem, (h, d - 1), y_peer[d])

    def rz_send(h, d):
        return remote(rs_z.at[h, zz[d]], rs_zr.at[h, d - 1], rz_sem, (h, d - 1), z_peer[d])

    def dq_store(h):
        cols = pl.ds(pl.multiple_of(h * (GROUP * HD), GROUP * HD), GROUP * HD)
        return pltpu.make_async_copy(dq.at[:, cols], dq_hbm.at[:, cols], dq_sem.at[h])

    def finish(slot):
        for plane in range(2):
            for a in range(NY):
                for b in range(NZ):
                    at = dst_tbl[plane * (NY * NZ) + a * NZ + b]
                    rs_full[slot, plane, a, b, 0] = (dk_acc[at] * SCALE).astype(bf16)
                    rs_full[slot, plane, a, b, 1] = dv_acc[at].astype(bf16)

    def start_rc(h):
        rc_send(h).start()
        dq_store(h).start()

    def reduce_core(slot):
        for a in range(NY):
            rs_y[slot, a] = (rs_full[slot, k, a].astype(f32) + rs_sib[slot, a].astype(f32)).astype(bf16)

    def start_ry(h):
        for d in range(1, NY):
            ry_send(h, d).start()

    def wait_ry(h):
        for d in range(1, NY):
            ry_send(h, d).wait_recv()

    def reduce_y(slot):
        total = rs_y[slot, y].astype(f32)
        for d in range(1, NY):
            total = total + rs_yr[slot, d - 1].astype(f32)
        rs_z[slot] = total.astype(bf16)

    def start_rz(h):
        for d in range(1, NZ):
            rz_send(h, d).start()

    def wait_rz(h):
        for d in range(1, NZ):
            rz_send(h, d).wait_recv()

    def reduce_z(slot):
        total = rs_z[slot, z].astype(f32)
        for d in range(1, NZ):
            total = total + rs_zr[slot, d - 1].astype(f32)
        sums[slot] = total

    for h in range(AHEAD):
        start_y(h)
        if h == 0:
            prepare()
    start_c(0)
    for h in range(Z_FIRST, KVH):
        start_column(h)
    q_load.wait()
    g_load.wait()
    c_recv(0).wait_recv()
    compact(0)
    front(0, 0, 0)

    def step(h, _):
        def late(lag):
            return jnp.where(h >= lag, h - lag, SPARE)

        @pl.when(h < Z_FIRST - 1)
        def _():
            start_c(h + 1)

        @pl.when(jnp.logical_and(h >= Z_FIRST - 1, h < KVH - 1))
        def _():
            start_c_late(h + 1)

        @pl.when(h >= 2)
        def _():
            rc_send(h - 2).wait_recv()

        @pl.when(h >= 4)
        def _():
            wait_ry(h - 4)

        @pl.when(h >= 6)
        def _():
            wait_rz(h - 6)

        front(h, 1, 1)
        middle(0)
        back(jnp.maximum(h - 1, 0), 3, 1, False)
        finish(late(1))
        reduce_core(late(2))
        reduce_y(late(4))
        reduce_z(late(6))

        @pl.when(h < Z_FIRST - AHEAD)
        def _():
            start_y(h + AHEAD)

        @pl.when(h >= 1)
        def _():
            start_rc(h - 1)

        @pl.when(h >= 2)
        def _():
            start_ry(h - 2)

        @pl.when(h >= 4)
        def _():
            start_rz(h - 4)

        transpose_keys()
        front(h, 2, 0)
        middle(1)
        back(h, 0, 0, True)
        front(h, 3, 1)
        middle(0)
        back(h, 1, 1, False)

        @pl.when(h < KVH - 1)
        def _():
            c_recv(h + 1).wait_recv()

        compact(jnp.minimum(h + 1, KVH - 1))
        front(jnp.minimum(h + 1, KVH - 1), 0, 0)
        middle(1)
        back(h, 2, 0, False)
        return 0

    lax.fori_loop(0, KVH, step, 0)
    last = KVH - 1
    rc_send(last - 1).wait_recv()
    reduce_core(last - 1)
    start_ry(last - 1)
    back(last, 3, 1, False)
    finish(last)
    start_rc(last)
    wait_ry(last - 3)
    reduce_y(last - 3)
    start_rz(last - 3)
    rc_send(last).wait_recv()
    reduce_core(last)
    start_ry(last)
    for h in (last - 2, last - 1):
        wait_ry(h)
        reduce_y(h)
        start_rz(h)
    for h in (last - 5, last - 4, last - 3, last - 2):
        wait_rz(h)
        reduce_z(h)
    wait_ry(last)
    reduce_y(last)
    start_rz(last)
    wait_rz(last - 1)
    reduce_z(last - 1)
    for h in range(last):
        dk_out[:, h * HD : (h + 1) * HD] = sums[h, 0]
        dv_out[:, h * HD : (h + 1) * HD] = sums[h, 1]
    wait_rz(last)
    reduce_z(last)
    dk_out[:, last * HD :] = sums[last, 0]
    dv_out[:, last * HD :] = sums[last, 1]

    def drain(h, _):
        @pl.when(h < Z_FIRST)
        def _():
            for d in range(1, NZ):
                z_send(h, d).wait_send()
            for d in range(1, NY):
                y_send(h, d).wait_send()

        @pl.when(h >= Z_FIRST)
        def _():
            for d in range(1, NZ):
                column_send(h, d).wait_send()
            for d in range(1, NY):
                block_send(h, d).wait_send()

        for d in range(1, NY):
            ry_send(h, d).wait_send()
        for d in range(1, NZ):
            rz_send(h, d).wait_send()
        c_send(h).wait_send()
        rc_send(h).wait_send()
        dq_store(h).wait()
        return 0

    lax.fori_loop(0, KVH, drain, 0)


def hand_out(dq, dk, dv, dq_out, dk_out, dv_out):
    dq_out[...] = dq[...]

    @pl.when(pl.program_id(0) == 0)
    def _():
        dk_out[...] = dk[...]
        dv_out[...] = dv[...]


def body(queries, out_grad, image_keys, image_values, link_ids, token_counts, tile_mask):
    smem = pl.BlockSpec(memory_space=pltpu.SMEM)
    vmem = pl.BlockSpec(memory_space=pltpu.VMEM)
    hbm = pl.BlockSpec(memory_space=pl.ANY)
    dma = pltpu.SemaphoreType.DMA
    lanes = 2 * TILE
    scratch = [
        pltpu.VMEM((TILE, H * HD), bf16),
        pltpu.VMEM((TILE, H * HD), bf16),
        pltpu.VMEM((TILE, H * HD), bf16),
        pltpu.VMEM((KVH, 2, NY, NZ, 2, ROWS, HD), bf16),
        pltpu.VMEM((BLOCKS, 2, ROWS, HD), bf16),
        pltpu.VMEM((LIVE, ROWS, 2 * HD), bf16),
        pltpu.VMEM((LIVE, ROWS, HD), bf16),
        pltpu.VMEM((HD, L), bf16),
        pltpu.VMEM((L, lanes), f32),
        pltpu.VMEM((L, lanes), f32),
        pltpu.VMEM((L, lanes), f32),
        pltpu.VMEM((L, lanes), f32),
        pltpu.VMEM((L, lanes), f32),
        pltpu.VMEM((L, lanes), bf16),
        pltpu.VMEM((L, lanes), bf16),
        pltpu.VMEM((L, lanes), bf16),
        pltpu.VMEM((L, lanes), bf16),
        pltpu.VMEM((LIVE + 1, ROWS, HD), f32),
        pltpu.VMEM((LIVE + 1, ROWS, HD), f32),
        pltpu.VMEM((KVH + 1, 2, NY, NZ, 2, ROWS, HD), bf16),
        pltpu.VMEM((KVH + 1, NY, NZ, 2, ROWS, HD), bf16),
        pltpu.VMEM((KVH + 1, NY, NZ, 2, ROWS, HD), bf16),
        pltpu.VMEM((KVH + 1, NY - 1, NZ, 2, ROWS, HD), bf16),
        pltpu.VMEM((KVH + 1, NZ, 2, ROWS, HD), bf16),
        pltpu.VMEM((KVH + 1, NZ - 1, 2, ROWS, HD), bf16),
        pltpu.VMEM((KVH + 1, 2, ROWS, HD), f32),
        pltpu.SMEM((LIVE,), jnp.int32),
        pltpu.SMEM((BLOCKS,), jnp.int32),
        pltpu.SMEM((LIVE,), jnp.int32),
        dma((2,)),
        dma((KVH,)),
        dma((KVH, NZ - 1)),
        dma((KVH, NZ - 1)),
        dma((KVH, NY - 1)),
        dma((KVH, NY - 1)),
        dma((KVH,)),
        dma((KVH,)),
        dma((KVH,)),
        dma((KVH,)),
        dma((KVH, NY - 1)),
        dma((KVH, NY - 1)),
        dma((KVH, NZ - 1)),
        dma((KVH, NZ - 1)),
    ]
    results = pl.pallas_call(
        kernel,
        out_shape=(
            jax.ShapeDtypeStruct((TILE, H * HD), bf16),
            jax.ShapeDtypeStruct((ROWS, KVH * HD), f32),
            jax.ShapeDtypeStruct((ROWS, KVH * HD), f32),
        ),
        in_specs=[smem, smem, smem, hbm, hbm, vmem, vmem],
        out_specs=[hbm, vmem, vmem],
        scratch_shapes=scratch,
        compiler_params=pltpu.CompilerParams(
            collective_id=0, has_side_effects=True, vmem_limit_bytes=56 << 20
        ),
        cost_estimate=pl.CostEstimate(
            flops=5 * 2 * TILE * H * L * HD, bytes_accessed=8 << 20, transcendentals=TILE * H * L
        ),
    )(link_ids, token_counts, tile_mask.T, queries, out_grad, image_keys, image_values)
    wide = pl.BlockSpec((TILE, H * HD // HAND_STEPS), lambda i: (0, i))
    whole = pl.BlockSpec((ROWS, KVH * HD), lambda i: (0, 0))
    specs = [wide, whole, whole]
    return pl.pallas_call(
        hand_out,
        out_shape=tuple(jax.ShapeDtypeStruct(r.shape, r.dtype) for r in results),
        grid=(HAND_STEPS,),
        in_specs=specs,
        out_specs=specs,
    )(*results)


def solution(mesh):
    rows = P(("dp", "context"), None)
    return jax.shard_map(
        body,
        mesh=mesh,
        in_specs=(rows, rows, rows, rows, P("dp"), P("dp"), P("dp", None)),
        out_specs=(rows, rows, rows),
        check_vma=False,
    )
```

```python
import functools
import math

import jax
import jax.numpy as jnp
from jax import lax
from jax.experimental import pallas as pl
from jax.experimental.pallas import tpu as pltpu
from jax.sharding import PartitionSpec as P

H = 64
KVH = 8
HD = 128
TILE = 128
IMAGES = 4
VIS = 256
GROUP = H // KVH
PAIRS = GROUP // 2
NY = 4
NZ = 8
ROWS = 16
BLOCKS = IMAGES * VIS // ROWS
LIVE = 42
L = LIVE * ROWS
CHUNK = 112
SCALE = 1.0 / math.sqrt(HD)
SCALE2 = SCALE * math.log2(math.e)
NEG = -1e30
HAND_STEPS = 8
Z_FIRST = 5
AHEAD = 4
SPARE = KVH
MESH = pl.DeviceIdType.MESH
f32 = jnp.float32
bf16 = jnp.bfloat16


def dot(a, b, ca, cb):
    return lax.dot_general(a, b, (((ca,), (cb,)), ((), ())), preferred_element_type=f32)


def device(y, z, k):
    return {"context": (y * NZ + z) * 2 + k}


def remote(src, dst, sems, at, target):
    send, recv = sems
    return pltpu.make_async_remote_copy(
        src_ref=src,
        dst_ref=dst,
        send_sem=send.at[at],
        recv_sem=recv.at[at],
        device_id=target,
        device_id_type=MESH,
    )


def kernel(
    links, counts, tiles, q_hbm, g_hbm, k_in, v_in,
    dq_hbm, dk_out, dv_out,
    q, g, dq, kv, cur, kaug, vc, kt, s0, s1, d0, d1, e_buf, p0, p1, w0, w1, dk_acc, dv_acc,
    rs_full, rs_sib, rs_y, rs_yr, rs_z, rs_zr, sums, src_tbl, dst_tbl, row_tbl,
    load_sem, dq_sem, zs, zr, ys, yr, cs, cr, rcs, rcr, rys, ryr, rzs, rzr,
):
    c = lax.axis_index("context")
    y, z, k = c // (2 * NZ), lax.rem(c // 2, NZ), lax.rem(c, 2)
    other = 1 - k
    yy = [lax.rem(y + d, NY) for d in range(NY)]
    zz = [lax.rem(z + d, NZ) for d in range(NZ)]
    sibling = device(y, z, other)
    y_peer = [device(yy[d], z, k) for d in range(NY)]
    z_peer = [device(y, zz[d], k) for d in range(NZ)]
    z_sem, y_sem, c_sem = (zs, zr), (ys, yr), (cs, cr)
    rc_sem, ry_sem, rz_sem = (rcs, rcr), (rys, ryr), (rzs, rzr)

    q_load = pltpu.make_async_copy(q_hbm, q, load_sem.at[0])
    g_load = pltpu.make_async_copy(g_hbm, g, load_sem.at[1])
    q_load.start()
    g_load.start()

    barrier = pltpu.get_barrier_semaphore()
    peers = [sibling] + y_peer[1:] + z_peer[1:]
    for peer in peers:
        pl.semaphore_signal(barrier, inc=1, device_id=peer, device_id_type=MESH)
    for h in range(KVH):
        kv[h, k, y, z, 0] = k_in[:, h * HD : (h + 1) * HD]
        kv[h, k, y, z, 1] = v_in[:, h * HD : (h + 1) * HD]
    pl.semaphore_wait(barrier, len(peers))

    def z_send(h, d):
        return remote(kv.at[h, k, y, z], kv.at[h, k, y, z], z_sem, (h, d - 1), z_peer[d])

    def z_recv(h, d):
        return remote(kv.at[h, k, y, z], kv.at[h, k, y, zz[NZ - d]], z_sem, (h, d - 1), z_peer[d])

    def y_send(h, d):
        return remote(kv.at[h, k, y], kv.at[h, k, y], y_sem, (h, d - 1), y_peer[d])

    def y_recv(h, d):
        return remote(kv.at[h, k, y], kv.at[h, k, yy[NY - d]], y_sem, (h, d - 1), y_peer[d])

    def c_send(h):
        return remote(kv.at[h, k], kv.at[h, k], c_sem, (h,), sibling)

    def c_recv(h):
        return remote(kv.at[h, k], kv.at[h, other], c_sem, (h,), sibling)

    def block_send(h, d):
        return remote(kv.at[h, k, y, z], kv.at[h, k, y, z], y_sem, (h, d - 1), y_peer[d])

    def block_recv(h, d):
        return remote(kv.at[h, k, y, z], kv.at[h, k, yy[NY - d], z], y_sem, (h, d - 1), y_peer[d])

    def column_send(h, d):
        return remote(kv.at[h, k, :, z], kv.at[h, k, :, z], z_sem, (h, d - 1), z_peer[d])

    def column_recv(h, d):
        return remote(kv.at[h, k, :, z], kv.at[h, k, :, zz[NZ - d]], z_sem, (h, d - 1), z_peer[d])

    def start_column(h):
        for d in range(1, NY):
            block_recv(h, d).wait_recv()
        for d in range(1, NZ):
            column_send(h, d).start()

    def start_y(h):
        for d in range(1, NZ):
            z_recv(h, d).wait_recv()
        for d in range(1, NY):
            y_send(h, d).start()

    def start_c(h):
        for d in range(1, NY):
            y_recv(h, d).wait_recv()
        c_send(h).start()

    def start_c_late(h):
        for d in range(1, NZ):
            column_recv(h, d).wait_recv()
        c_send(h).start()

    for h in range(KVH):
        if h < Z_FIRST:
            for d in range(1, NZ):
                z_send(h, d).start()
        else:
            for d in range(1, NY):
                block_send(h, d).start()

    def prepare():
        zero = jnp.int32(0)
        live_rows, first_block = [], [zero]
        for image in range(IMAGES):
            seen = zero
            for p in range(IMAGES):
                seen = seen + jnp.where(links[p] == image, tiles[p, c], 0)
            live_rows.append(jnp.where(seen > 0, counts[image], 0))
            first_block.append(first_block[-1] + (live_rows[-1] + (ROWS - 1)) // ROWS)
        spare = first_block[IMAGES]

        def fill_src(b, _):
            image, base, rows = zero, zero, live_rows[0]
            for i in range(1, IMAGES):
                past = b >= first_block[i]
                image = jnp.where(past, i, image)
                base = jnp.where(past, first_block[i], base)
                rows = jnp.where(past, live_rows[i], rows)
            u = jnp.minimum(b - base, VIS // ROWS - 1)
            src_tbl[b] = lax.rem(u, 2) * (NY * NZ) + image * NZ + u // 2
            row_tbl[b] = jnp.where(b < spare, rows - (b - base) * ROWS, 0)
            return 0

        lax.fori_loop(0, LIVE, fill_src, 0)
        for image in range(IMAGES):

            def fill_dst(u, _):
                at = lax.rem(u, 2) * (NY * NZ) + image * NZ + u // 2
                dst_tbl[at] = jnp.where(u * ROWS < live_rows[image], first_block[image] + u, LIVE)
                return 0

            lax.fori_loop(0, VIS // ROWS, fill_dst, 0)

        lane = lax.broadcasted_iota(jnp.int32, (ROWS, HD), 1)
        row = lax.broadcasted_iota(jnp.int32, (ROWS, HD), 0)

        def fill_bias(b, _):
            dead = jnp.logical_and(lane == 0, row >= row_tbl[b])
            kaug[b, :, HD:] = jnp.where(dead, NEG, 0.0).astype(bf16)
            return 0

        lax.fori_loop(0, LIVE, fill_bias, 0)
        dk_acc[LIVE] = jnp.zeros((ROWS, HD), f32)
        dv_acc[LIVE] = jnp.zeros((ROWS, HD), f32)

    def compact(h):
        flat = 2 * NY * NZ
        cur[...] = kv[h].reshape(flat, 2, ROWS, HD)
        for b in range(LIVE):
            kaug[b, :, :HD] = cur[src_tbl[b], 0]
            vc[b] = cur[src_tbl[b], 1]

    def transpose_keys(h):
        kt[h] = kaug[...].reshape(L, 2 * HD)[:, :HD].T

    s_buf, d_buf, p_buf, w_buf = (s0, s1), (d0, d1), (p0, p1), (w0, w1)
    ones = jnp.where(lax.broadcasted_iota(jnp.int32, (2 * TILE, HD), 1) == 0, 1.0, 0.0).astype(bf16)

    def two_heads(ref, h, pair):
        start = pl.multiple_of(h * (GROUP * HD) + pair * (2 * HD), 2 * HD)
        both = ref[:, pl.ds(start, 2 * HD)]
        return jnp.concatenate([both[:, :HD], both[:, HD:]], axis=0)

    def front(h, pair, slot):
        rows_q = jnp.concatenate([two_heads(q, h, pair), ones], axis=1)
        s_buf[slot][...] = dot(kaug[...].reshape(L, 2 * HD), rows_q, 1, 1)
        d_buf[slot][...] = dot(vc[...].reshape(L, HD), two_heads(g, h, pair), 1, 1)

    def middle(h, pair):
        slot, to = pair % 2, h * 2 + pair // 2
        tops, sums, deltas = [], [], []
        lanes = 2 * TILE
        for i in range(L // CHUNK):
            at = slice(i * CHUNK, (i + 1) * CHUNK)
            s = s_buf[slot][at, :]
            top = jnp.max(s, axis=0, keepdims=True) * SCALE2
            e = jnp.exp2(s * SCALE2 - top)
            e_buf[at, :] = e
            sums.append(jnp.sum(e.reshape(CHUNK // 8, 8, lanes), axis=0))
            deltas.append(jnp.sum((e * d_buf[slot][at, :]).reshape(CHUNK // 8, 8, lanes), axis=0))
            tops.append(top)
        top = functools.reduce(jnp.maximum, tops)
        weight = [jnp.exp2(t - top) for t in tops]
        total = jnp.sum(sum(a * b for a, b in zip(sums, weight)), axis=0, keepdims=True)
        delta = jnp.sum(sum(a * b for a, b in zip(deltas, weight)), axis=0, keepdims=True)
        inverse = 1.0 / total
        delta = delta * inverse
        for i in range(L // CHUNK):
            at = slice(i * CHUNK, (i + 1) * CHUNK)
            prob = e_buf[at, :] * (weight[i] * inverse)
            p_buf[slot][at, :] = prob.astype(bf16)
            w_buf[slot][to, at, :] = (prob * (d_buf[slot][at, :] - delta)).astype(bf16)

    def query_terms(h, pair):
        dqt = dot(kt[h], w_buf[pair % 2][h * 2 + pair // 2], 1, 0) * SCALE
        for j in range(2):
            start = pl.multiple_of(h * (GROUP * HD) + pair * (2 * HD) + j * HD, HD)
            dq[:, pl.ds(start, HD)] = dqt[:, j * TILE : (j + 1) * TILE].T.astype(bf16)

    def query_grads(first, number):
        def one(h, _):
            for pair in range(PAIRS):
                query_terms(h, pair)
            dq_store(h).start()
            return 0

        lax.fori_loop(first, first + number, one, 0)

    def back(h, pair, slot, first):
        dv = dot(p_buf[slot][...], two_heads(g, h, pair), 1, 0).reshape(LIVE, ROWS, HD)
        dk = dot(w_buf[slot][h * 2 + pair // 2], two_heads(q, h, pair), 1, 0).reshape(LIVE, ROWS, HD)
        if first:
            dv_acc[:LIVE] = dv
            dk_acc[:LIVE] = dk
        else:
            dv_acc[:LIVE] += dv
            dk_acc[:LIVE] += dk

    def rc_send(h):
        return remote(rs_full.at[h, other], rs_sib.at[h], rc_sem, (h,), sibling)

    def ry_send(h, d):
        return remote(rs_y.at[h, yy[d]], rs_yr.at[h, d - 1], ry_sem, (h, d - 1), y_peer[d])

    def rz_send(h, d):
        return remote(rs_z.at[h, zz[d]], rs_zr.at[h, d - 1], rz_sem, (h, d - 1), z_peer[d])

    def dq_store(h):
        cols = pl.ds(pl.multiple_of(h * (GROUP * HD), GROUP * HD), GROUP * HD)
        return pltpu.make_async_copy(dq.at[:, cols], dq_hbm.at[:, cols], dq_sem.at[h])

    def finish(slot):
        for plane in range(2):
            for a in range(NY):
                for b in range(NZ):
                    at = dst_tbl[plane * (NY * NZ) + a * NZ + b]
                    rs_full[slot, plane, a, b, 0] = (dk_acc[at] * SCALE).astype(bf16)
                    rs_full[slot, plane, a, b, 1] = dv_acc[at].astype(bf16)

    def start_rc(h):
        rc_send(h).start()

    def reduce_core(slot):
        for a in range(NY):
            rs_y[slot, a] = (rs_full[slot, k, a].astype(f32) + rs_sib[slot, a].astype(f32)).astype(bf16)

    def start_ry(h):
        for d in range(1, NY):
            ry_send(h, d).start()

    def wait_ry(h):
        for d in range(1, NY):
            ry_send(h, d).wait_recv()

    def reduce_y(slot):
        total = rs_y[slot, y].astype(f32)
        for d in range(1, NY):
            total = total + rs_yr[slot, d - 1].astype(f32)
        rs_z[slot] = total.astype(bf16)

    def start_rz(h):
        for d in range(1, NZ):
            rz_send(h, d).start()

    def wait_rz(h):
        for d in range(1, NZ):
            rz_send(h, d).wait_recv()

    def reduce_z(slot):
        total = rs_z[slot, z].astype(f32)
        for d in range(1, NZ):
            total = total + rs_zr[slot, d - 1].astype(f32)
        sums[slot] = total

    prepare()
    for h in range(AHEAD):
        start_y(h)
    start_c(0)
    for h in range(Z_FIRST, KVH):
        start_column(h)
    q_load.wait()
    g_load.wait()
    c_recv(0).wait_recv()
    compact(0)
    front(0, 0, 0)

    def step(h, _):
        def late(lag):
            return jnp.where(h >= lag, h - lag, SPARE)

        @pl.when(h < Z_FIRST - 1)
        def _():
            start_c(h + 1)

        @pl.when(jnp.logical_and(h >= Z_FIRST - 1, h < KVH - 1))
        def _():
            start_c_late(h + 1)

        @pl.when(h >= 2)
        def _():
            rc_send(h - 2).wait_recv()

        @pl.when(h >= 4)
        def _():
            wait_ry(h - 4)

        @pl.when(h >= 6)
        def _():
            wait_rz(h - 6)

        front(h, 1, 1)
        middle(h, 0)
        back(jnp.maximum(h - 1, 0), 3, 1, False)
        finish(late(1))
        reduce_core(late(2))
        reduce_y(late(4))
        reduce_z(late(6))

        @pl.when(h < Z_FIRST - AHEAD)
        def _():
            start_y(h + AHEAD)

        @pl.when(h >= 1)
        def _():
            start_rc(h - 1)

        @pl.when(h >= 2)
        def _():
            start_ry(h - 2)

        @pl.when(h >= 4)
        def _():
            start_rz(h - 4)

        transpose_keys(h)
        front(h, 2, 0)
        middle(h, 1)
        back(h, 0, 0, True)
        front(h, 3, 1)
        middle(h, 2)
        back(h, 1, 1, False)

        @pl.when(h < KVH - 1)
        def _():
            c_recv(h + 1).wait_recv()

        compact(jnp.minimum(h + 1, KVH - 1))
        front(jnp.minimum(h + 1, KVH - 1), 0, 0)
        middle(h, 3)
        back(h, 2, 0, False)
        return 0

    lax.fori_loop(0, KVH, step, 0)
    last = KVH - 1
    rc_send(last - 1).wait_recv()
    reduce_core(last - 1)
    start_ry(last - 1)
    back(last, 3, 1, False)
    finish(last)
    start_rc(last)
    wait_ry(last - 3)
    reduce_y(last - 3)
    start_rz(last - 3)
    rc_send(last).wait_recv()
    reduce_core(last)
    start_ry(last)
    query_grads(0, 3)
    for h in (last - 2, last - 1):
        wait_ry(h)
        reduce_y(h)
        start_rz(h)
    query_grads(3, 2)
    for h in (last - 5, last - 4, last - 3, last - 2):
        wait_rz(h)
        reduce_z(h)
    wait_ry(last)
    reduce_y(last)
    start_rz(last)
    query_grads(5, 3)
    wait_rz(last - 1)
    reduce_z(last - 1)
    for h in range(last):
        dk_out[:, h * HD : (h + 1) * HD] = sums[h, 0]
        dv_out[:, h * HD : (h + 1) * HD] = sums[h, 1]
    wait_rz(last)
    reduce_z(last)
    dk_out[:, last * HD :] = sums[last, 0]
    dv_out[:, last * HD :] = sums[last, 1]

    def drain(h, _):
        @pl.when(h < Z_FIRST)
        def _():
            for d in range(1, NZ):
                z_send(h, d).wait_send()
            for d in range(1, NY):
                y_send(h, d).wait_send()

        @pl.when(h >= Z_FIRST)
        def _():
            for d in range(1, NZ):
                column_send(h, d).wait_send()
            for d in range(1, NY):
                block_send(h, d).wait_send()

        for d in range(1, NY):
            ry_send(h, d).wait_send()
        for d in range(1, NZ):
            rz_send(h, d).wait_send()
        c_send(h).wait_send()
        rc_send(h).wait_send()
        dq_store(h).wait()
        return 0

    lax.fori_loop(0, KVH, drain, 0)


def hand_out(dq, dk, dv, dq_out, dk_out, dv_out, dq_mid, dk_mid, dv_mid, sems):
    width = H * HD // HAND_STEPS
    steps = [pl.ds(i * width, width) for i in range(HAND_STEPS)]
    parts = [(dk, dk_mid, dk_out), (dv, dv_mid, dv_out)]
    parts += [(dq.at[:, at], dq_mid.at[:, at], dq_out.at[:, at]) for at in steps]
    reads = [pltpu.make_async_copy(a, b, sems.at[0, i]) for i, (a, b, _) in enumerate(parts)]
    writes = [pltpu.make_async_copy(b, c, sems.at[1, i]) for i, (_, b, c) in enumerate(parts)]
    for copy in reads:
        copy.start()
    for read, write in zip(reads, writes):
        read.wait()
        write.start()
    for copy in writes:
        copy.wait()


def body(queries, out_grad, image_keys, image_values, link_ids, token_counts, tile_mask):
    smem = pl.BlockSpec(memory_space=pltpu.SMEM)
    vmem = pl.BlockSpec(memory_space=pltpu.VMEM)
    hbm = pl.BlockSpec(memory_space=pl.ANY)
    dma = pltpu.SemaphoreType.DMA
    lanes = 2 * TILE
    scratch = [
        pltpu.VMEM((TILE, H * HD), bf16),
        pltpu.VMEM((TILE, H * HD), bf16),
        pltpu.VMEM((TILE, H * HD), bf16),
        pltpu.VMEM((KVH, 2, NY, NZ, 2, ROWS, HD), bf16),
        pltpu.VMEM((BLOCKS, 2, ROWS, HD), bf16),
        pltpu.VMEM((LIVE, ROWS, 2 * HD), bf16),
        pltpu.VMEM((LIVE, ROWS, HD), bf16),
        pltpu.VMEM((KVH, HD, L), bf16),
        pltpu.VMEM((L, lanes), f32),
        pltpu.VMEM((L, lanes), f32),
        pltpu.VMEM((L, lanes), f32),
        pltpu.VMEM((L, lanes), f32),
        pltpu.VMEM((L, lanes), f32),
        pltpu.VMEM((L, lanes), bf16),
        pltpu.VMEM((L, lanes), bf16),
        pltpu.VMEM((KVH * PAIRS // 2, L, lanes), bf16),
        pltpu.VMEM((KVH * PAIRS // 2, L, lanes), bf16),
        pltpu.VMEM((LIVE + 1, ROWS, HD), f32),
        pltpu.VMEM((LIVE + 1, ROWS, HD), f32),
        pltpu.VMEM((KVH + 1, 2, NY, NZ, 2, ROWS, HD), bf16),
        pltpu.VMEM((KVH + 1, NY, NZ, 2, ROWS, HD), bf16),
        pltpu.VMEM((KVH + 1, NY, NZ, 2, ROWS, HD), bf16),
        pltpu.VMEM((KVH + 1, NY - 1, NZ, 2, ROWS, HD), bf16),
        pltpu.VMEM((KVH + 1, NZ, 2, ROWS, HD), bf16),
        pltpu.VMEM((KVH + 1, NZ - 1, 2, ROWS, HD), bf16),
        pltpu.VMEM((KVH + 1, 2, ROWS, HD), f32),
        pltpu.SMEM((LIVE,), jnp.int32),
        pltpu.SMEM((BLOCKS,), jnp.int32),
        pltpu.SMEM((LIVE,), jnp.int32),
        dma((2,)),
        dma((KVH,)),
        dma((KVH, NZ - 1)),
        dma((KVH, NZ - 1)),
        dma((KVH, NY - 1)),
        dma((KVH, NY - 1)),
        dma((KVH,)),
        dma((KVH,)),
        dma((KVH,)),
        dma((KVH,)),
        dma((KVH, NY - 1)),
        dma((KVH, NY - 1)),
        dma((KVH, NZ - 1)),
        dma((KVH, NZ - 1)),
    ]
    results = pl.pallas_call(
        kernel,
        out_shape=(
            jax.ShapeDtypeStruct((TILE, H * HD), bf16),
            jax.ShapeDtypeStruct((ROWS, KVH * HD), f32),
            jax.ShapeDtypeStruct((ROWS, KVH * HD), f32),
        ),
        in_specs=[smem, smem, smem, hbm, hbm, vmem, vmem],
        out_specs=[hbm, vmem, vmem],
        scratch_shapes=scratch,
        compiler_params=pltpu.CompilerParams(
            collective_id=0, has_side_effects=True, vmem_limit_bytes=56 << 20
        ),
        cost_estimate=pl.CostEstimate(
            flops=5 * 2 * TILE * H * L * HD, bytes_accessed=8 << 20, transcendentals=TILE * H * L
        ),
    )(link_ids, token_counts, tile_mask.T, queries, out_grad, image_keys, image_values)
    return pl.pallas_call(
        hand_out,
        out_shape=tuple(jax.ShapeDtypeStruct(r.shape, r.dtype) for r in results),
        in_specs=[hbm] * 3,
        out_specs=[hbm] * 3,
        scratch_shapes=[pltpu.VMEM(r.shape, r.dtype) for r in results] + [dma((2, HAND_STEPS + 2))],
    )(*results)


def solution(mesh):
    rows = P(("dp", "context"), None)
    return jax.shard_map(
        body,
        mesh=mesh,
        in_specs=(rows, rows, rows, rows, P("dp"), P("dp"), P("dp", None)),
        out_specs=(rows, rows, rows),
        check_vma=False,
    )
```

```python
import functools
import math

import jax
import jax.numpy as jnp
from jax import lax
from jax.experimental import pallas as pl
from jax.experimental.pallas import tpu as pltpu
from jax.sharding import PartitionSpec as P

H = 64
KVH = 8
HD = 128
TILE = 128
IMAGES = 4
VIS = 256
GROUP = H // KVH
PAIRS = GROUP // 2
NY = 4
NZ = 8
ROWS = 16
BLOCKS = IMAGES * VIS // ROWS
LIVE = 42
L = LIVE * ROWS
CHUNK = 112
SCALE = 1.0 / math.sqrt(HD)
SCALE2 = SCALE * math.log2(math.e)
NEG = -1e30
HAND_STEPS = 8
Z_FIRST = 5
AHEAD = 4
SPARE = KVH
MESH = pl.DeviceIdType.MESH
f32 = jnp.float32
bf16 = jnp.bfloat16


def dot(a, b, ca, cb):
    return lax.dot_general(a, b, (((ca,), (cb,)), ((), ())), preferred_element_type=f32)


def device(y, z, k):
    return {"context": (y * NZ + z) * 2 + k}


def remote(src, dst, sems, at, target):
    send, recv = sems
    return pltpu.make_async_remote_copy(
        src_ref=src,
        dst_ref=dst,
        send_sem=send.at[at],
        recv_sem=recv.at[at],
        device_id=target,
        device_id_type=MESH,
    )


def kernel(
    links, counts, tiles, q_hbm, g_hbm, k_in, v_in,
    dq_hbm, dk_out, dv_out,
    q, g, dq, kv, cur, kaug, vc, kt, s0, s1, d0, d1, e_buf, p0, p1, w0, w1, dk_acc, dv_acc,
    rs_full, rs_sib, rs_y, rs_yr, rs_z, rs_zr, sums, src_tbl, dst_tbl, row_tbl,
    load_sem, dq_sem, ws, wr, zs, zr, ys, yr, cs, cr, rcs, rcr, rys, ryr, rzs, rzr,
):
    c = lax.axis_index("context")
    y, z, k = c // (2 * NZ), lax.rem(c // 2, NZ), lax.rem(c, 2)
    other = 1 - k
    yy = [lax.rem(y + d, NY) for d in range(NY)]
    zz = [lax.rem(z + d, NZ) for d in range(NZ)]
    sibling = device(y, z, other)
    y_peer = [device(yy[d], z, k) for d in range(NY)]
    z_peer = [device(y, zz[d], k) for d in range(NZ)]
    z_sem, y_sem, c_sem, row_sem = (zs, zr), (ys, yr), (cs, cr), (ws, wr)
    rc_sem, ry_sem, rz_sem = (rcs, rcr), (rys, ryr), (rzs, rzr)

    q_load = pltpu.make_async_copy(q_hbm, q, load_sem.at[0])
    g_load = pltpu.make_async_copy(g_hbm, g, load_sem.at[1])
    q_load.start()
    g_load.start()

    barrier = pltpu.get_barrier_semaphore()
    peers = [sibling] + y_peer[1:] + z_peer[1:]
    for peer in peers:
        pl.semaphore_signal(barrier, inc=1, device_id=peer, device_id_type=MESH)
    for h in range(KVH):
        kv[h, k, y, z, 0] = k_in[:, h * HD : (h + 1) * HD]
        kv[h, k, y, z, 1] = v_in[:, h * HD : (h + 1) * HD]
    pl.semaphore_wait(barrier, len(peers))

    def z_send(h, d):
        return remote(kv.at[h, k, y, z], kv.at[h, k, y, z], z_sem, (h, d - 1), z_peer[d])

    def z_recv(h, d):
        return remote(kv.at[h, k, y, z], kv.at[h, k, y, zz[NZ - d]], z_sem, (h, d - 1), z_peer[d])

    def y_send(h, d):
        return remote(kv.at[h, k, y], kv.at[h, k, y], y_sem, (h, d - 1), y_peer[d])

    def y_recv(h, d):
        return remote(kv.at[h, k, y], kv.at[h, k, yy[NY - d]], y_sem, (h, d - 1), y_peer[d])

    def c_send(h):
        return remote(kv.at[h, k], kv.at[h, k], c_sem, (h,), sibling)

    def row_send(d):
        row = kv.at[0, k, yy[d]]
        return remote(row, row, row_sem, (d,), sibling)

    def row_recv(d):
        return remote(kv.at[0, k, yy[d]], kv.at[0, other, yy[d]], row_sem, (d,), sibling)

    def c_recv(h):
        return remote(kv.at[h, k], kv.at[h, other], c_sem, (h,), sibling)

    def block_send(h, d):
        return remote(kv.at[h, k, y, z], kv.at[h, k, y, z], y_sem, (h, d - 1), y_peer[d])

    def block_recv(h, d):
        return remote(kv.at[h, k, y, z], kv.at[h, k, yy[NY - d], z], y_sem, (h, d - 1), y_peer[d])

    def column_send(h, d):
        return remote(kv.at[h, k, :, z], kv.at[h, k, :, z], z_sem, (h, d - 1), z_peer[d])

    def column_recv(h, d):
        return remote(kv.at[h, k, :, z], kv.at[h, k, :, zz[NZ - d]], z_sem, (h, d - 1), z_peer[d])

    def start_column(h):
        for d in range(1, NY):
            block_recv(h, d).wait_recv()
        for d in range(1, NZ):
            column_send(h, d).start()

    def start_y(h):
        for d in range(1, NZ):
            z_recv(h, d).wait_recv()
        for d in range(1, NY):
            y_send(h, d).start()

    def start_c(h):
        for d in range(1, NY):
            y_recv(h, d).wait_recv()
        c_send(h).start()

    def start_c_late(h):
        for d in range(1, NZ):
            column_recv(h, d).wait_recv()
        c_send(h).start()

    for h in range(KVH):
        if h < Z_FIRST:
            for d in range(1, NZ):
                z_send(h, d).start()
        else:
            for d in range(1, NY):
                block_send(h, d).start()

    def prepare():
        zero = jnp.int32(0)
        live_rows, first_block = [], [zero]
        for image in range(IMAGES):
            seen = zero
            for p in range(IMAGES):
                seen = seen + jnp.where(links[p] == image, tiles[p, c], 0)
            live_rows.append(jnp.where(seen > 0, counts[image], 0))
            first_block.append(first_block[-1] + (live_rows[-1] + (ROWS - 1)) // ROWS)
        spare = first_block[IMAGES]

        def fill_src(b, _):
            image, base, rows = zero, zero, live_rows[0]
            for i in range(1, IMAGES):
                past = b >= first_block[i]
                image = jnp.where(past, i, image)
                base = jnp.where(past, first_block[i], base)
                rows = jnp.where(past, live_rows[i], rows)
            u = jnp.minimum(b - base, VIS // ROWS - 1)
            src_tbl[b] = lax.rem(u, 2) * (NY * NZ) + image * NZ + u // 2
            row_tbl[b] = jnp.where(b < spare, rows - (b - base) * ROWS, 0)
            return 0

        lax.fori_loop(0, LIVE, fill_src, 0)
        for image in range(IMAGES):

            def fill_dst(u, _):
                at = lax.rem(u, 2) * (NY * NZ) + image * NZ + u // 2
                dst_tbl[at] = jnp.where(u * ROWS < live_rows[image], first_block[image] + u, LIVE)
                return 0

            lax.fori_loop(0, VIS // ROWS, fill_dst, 0)

        lane = lax.broadcasted_iota(jnp.int32, (ROWS, HD), 1)
        row = lax.broadcasted_iota(jnp.int32, (ROWS, HD), 0)

        def fill_bias(b, _):
            dead = jnp.logical_and(lane == 0, row >= row_tbl[b])
            kaug[b, :, HD:] = jnp.where(dead, NEG, 0.0).astype(bf16)
            return 0

        lax.fori_loop(0, LIVE, fill_bias, 0)
        dk_acc[LIVE] = jnp.zeros((ROWS, HD), f32)
        dv_acc[LIVE] = jnp.zeros((ROWS, HD), f32)

    def compact(h):
        flat = 2 * NY * NZ
        cur[...] = kv[h].reshape(flat, 2, ROWS, HD)
        for b in range(LIVE):
            kaug[b, :, :HD] = cur[src_tbl[b], 0]
            vc[b] = cur[src_tbl[b], 1]

    def transpose_keys(h):
        kt[h] = kaug[...].reshape(L, 2 * HD)[:, :HD].T

    s_buf, d_buf, p_buf, w_buf = (s0, s1), (d0, d1), (p0, p1), (w0, w1)
    ones = jnp.where(lax.broadcasted_iota(jnp.int32, (2 * TILE, HD), 1) == 0, 1.0, 0.0).astype(bf16)

    def two_heads(ref, h, pair):
        start = pl.multiple_of(h * (GROUP * HD) + pair * (2 * HD), 2 * HD)
        both = ref[:, pl.ds(start, 2 * HD)]
        return jnp.concatenate([both[:, :HD], both[:, HD:]], axis=0)

    def front(h, pair, slot):
        rows_q = jnp.concatenate([two_heads(q, h, pair), ones], axis=1)
        s_buf[slot][...] = dot(kaug[...].reshape(L, 2 * HD), rows_q, 1, 1)
        d_buf[slot][...] = dot(vc[...].reshape(L, HD), two_heads(g, h, pair), 1, 1)

    def middle(h, pair):
        slot, to = pair % 2, h * 2 + pair // 2
        tops, sums, deltas = [], [], []
        lanes = 2 * TILE
        for i in range(L // CHUNK):
            at = slice(i * CHUNK, (i + 1) * CHUNK)
            s = s_buf[slot][at, :]
            top = jnp.max(s, axis=0, keepdims=True) * SCALE2
            e = jnp.exp2(s * SCALE2 - top)
            e_buf[at, :] = e
            sums.append(jnp.sum(e.reshape(CHUNK // 8, 8, lanes), axis=0))
            deltas.append(jnp.sum((e * d_buf[slot][at, :]).reshape(CHUNK // 8, 8, lanes), axis=0))
            tops.append(top)
        top = functools.reduce(jnp.maximum, tops)
        weight = [jnp.exp2(t - top) for t in tops]
        total = jnp.sum(sum(a * b for a, b in zip(sums, weight)), axis=0, keepdims=True)
        delta = jnp.sum(sum(a * b for a, b in zip(deltas, weight)), axis=0, keepdims=True)
        inverse = 1.0 / total
        delta = delta * inverse
        for i in range(L // CHUNK):
            at = slice(i * CHUNK, (i + 1) * CHUNK)
            prob = e_buf[at, :] * (weight[i] * inverse)
            p_buf[slot][at, :] = prob.astype(bf16)
            w_buf[slot][to, at, :] = (prob * (d_buf[slot][at, :] - delta)).astype(bf16)

    def query_terms(h, pair):
        dqt = dot(kt[h], w_buf[pair % 2][h * 2 + pair // 2], 1, 0) * SCALE
        for j in range(2):
            start = pl.multiple_of(h * (GROUP * HD) + pair * (2 * HD) + j * HD, HD)
            dq[:, pl.ds(start, HD)] = dqt[:, j * TILE : (j + 1) * TILE].T.astype(bf16)

    def query_grads(first, number):
        def one(h, _):
            for pair in range(PAIRS):
                query_terms(h, pair)
            dq_store(h).start()
            return 0

        lax.fori_loop(first, first + number, one, 0)

    def back(h, pair, slot, first):
        dv = dot(p_buf[slot][...], two_heads(g, h, pair), 1, 0).reshape(LIVE, ROWS, HD)
        dk = dot(w_buf[slot][h * 2 + pair // 2], two_heads(q, h, pair), 1, 0).reshape(LIVE, ROWS, HD)
        if first:
            dv_acc[:LIVE] = dv
            dk_acc[:LIVE] = dk
        else:
            dv_acc[:LIVE] += dv
            dk_acc[:LIVE] += dk

    def rc_send(h):
        return remote(rs_full.at[h, other], rs_sib.at[h], rc_sem, (h,), sibling)

    def ry_send(h, d):
        return remote(rs_y.at[h, yy[d]], rs_yr.at[h, d - 1], ry_sem, (h, d - 1), y_peer[d])

    def rz_send(h, d):
        return remote(rs_z.at[h, zz[d]], rs_zr.at[h, d - 1], rz_sem, (h, d - 1), z_peer[d])

    def dq_store(h):
        cols = pl.ds(pl.multiple_of(h * (GROUP * HD), GROUP * HD), GROUP * HD)
        return pltpu.make_async_copy(dq.at[:, cols], dq_hbm.at[:, cols], dq_sem.at[h])

    def finish(slot):
        for plane in range(2):
            for a in range(NY):
                for b in range(NZ):
                    at = dst_tbl[plane * (NY * NZ) + a * NZ + b]
                    rs_full[slot, plane, a, b, 0] = (dk_acc[at] * SCALE).astype(bf16)
                    rs_full[slot, plane, a, b, 1] = dv_acc[at].astype(bf16)

    def start_rc(h):
        rc_send(h).start()

    def reduce_core(slot):
        for a in range(NY):
            rs_y[slot, a] = (rs_full[slot, k, a].astype(f32) + rs_sib[slot, a].astype(f32)).astype(bf16)

    def start_ry(h):
        for d in range(1, NY):
            ry_send(h, d).start()

    def wait_ry(h):
        for d in range(1, NY):
            ry_send(h, d).wait_recv()

    def reduce_y(slot):
        total = rs_y[slot, y].astype(f32)
        for d in range(1, NY):
            total = total + rs_yr[slot, d - 1].astype(f32)
        rs_z[slot] = total.astype(bf16)

    def start_rz(h):
        for d in range(1, NZ):
            rz_send(h, d).start()

    def wait_rz(h):
        for d in range(1, NZ):
            rz_send(h, d).wait_recv()

    def reduce_z(slot):
        total = rs_z[slot, z].astype(f32)
        for d in range(1, NZ):
            total = total + rs_zr[slot, d - 1].astype(f32)
        sums[slot] = total

    prepare()
    start_y(0)
    row_send(0).start()
    for h in range(Z_FIRST, KVH):
        start_column(h)
    for h in range(1, AHEAD):
        start_y(h)
    for d in (1, 3, 2):
        y_recv(0, d).wait_recv()
        row_send(NY - d).start()
    q_load.wait()
    g_load.wait()
    for d in range(NY):
        row_recv(d).wait_recv()
    compact(0)
    front(0, 0, 0)

    def step(h, _):
        def late(lag):
            return jnp.where(h >= lag, h - lag, SPARE)

        @pl.when(h < Z_FIRST - 1)
        def _():
            start_c(h + 1)

        @pl.when(jnp.logical_and(h >= Z_FIRST - 1, h < KVH - 1))
        def _():
            start_c_late(h + 1)

        @pl.when(h >= 2)
        def _():
            rc_send(h - 2).wait_recv()

        @pl.when(h >= 5)
        def _():
            wait_ry(h - 5)

        front(h, 1, 1)
        middle(h, 0)
        back(jnp.maximum(h - 1, 0), 3, 1, False)
        finish(late(1))
        reduce_core(late(2))
        reduce_y(late(5))

        @pl.when(h < Z_FIRST - AHEAD)
        def _():
            start_y(h + AHEAD)

        @pl.when(h >= 1)
        def _():
            start_rc(h - 1)

        @pl.when(h >= 2)
        def _():
            start_ry(h - 2)

        @pl.when(h >= 5)
        def _():
            start_rz(h - 5)

        transpose_keys(h)
        front(h, 2, 0)
        middle(h, 1)
        back(h, 0, 0, True)
        front(h, 3, 1)
        middle(h, 2)
        back(h, 1, 1, False)

        @pl.when(h < KVH - 1)
        def _():
            c_recv(h + 1).wait_recv()

        compact(jnp.minimum(h + 1, KVH - 1))
        front(jnp.minimum(h + 1, KVH - 1), 0, 0)
        middle(h, 3)
        back(h, 2, 0, False)
        return 0

    lax.fori_loop(0, KVH, step, 0)
    last = KVH - 1
    rc_send(last - 1).wait_recv()
    reduce_core(last - 1)
    start_ry(last - 1)
    back(last, 3, 1, False)
    finish(last)
    start_rc(last)
    for h in (last - 4, last - 3):
        wait_ry(h)
        reduce_y(h)
        start_rz(h)
    rc_send(last).wait_recv()
    reduce_core(last)
    start_ry(last)
    query_grads(0, 3)
    for h in (last - 2, last - 1):
        wait_ry(h)
        reduce_y(h)
        start_rz(h)
    query_grads(3, 2)
    for h in range(last - 2):
        wait_rz(h)
        reduce_z(h)
    wait_ry(last)
    reduce_y(last)
    start_rz(last)
    query_grads(5, 3)
    for h in (last - 2, last - 1):
        wait_rz(h)
        reduce_z(h)
    for h in range(last):
        dk_out[:, h * HD : (h + 1) * HD] = sums[h, 0]
        dv_out[:, h * HD : (h + 1) * HD] = sums[h, 1]
    wait_rz(last)
    reduce_z(last)
    dk_out[:, last * HD :] = sums[last, 0]
    dv_out[:, last * HD :] = sums[last, 1]

    def drain(h, _):
        @pl.when(h < Z_FIRST)
        def _():
            for d in range(1, NZ):
                z_send(h, d).wait_send()
            for d in range(1, NY):
                y_send(h, d).wait_send()

        @pl.when(h >= Z_FIRST)
        def _():
            for d in range(1, NZ):
                column_send(h, d).wait_send()
            for d in range(1, NY):
                block_send(h, d).wait_send()

        for d in range(1, NY):
            ry_send(h, d).wait_send()
        for d in range(1, NZ):
            rz_send(h, d).wait_send()
        @pl.when(h > 0)
        def _():
            c_send(h).wait_send()

        rc_send(h).wait_send()
        dq_store(h).wait()
        return 0

    lax.fori_loop(0, KVH, drain, 0)
    for d in range(NY):
        row_send(d).wait_send()


def hand_out(dq, dk, dv, dq_out, dk_out, dv_out, dq_mid, dk_mid, dv_mid, sems):
    width = H * HD // HAND_STEPS
    steps = [pl.ds(i * width, width) for i in range(HAND_STEPS)]
    parts = [(dk, dk_mid, dk_out), (dv, dv_mid, dv_out)]
    parts += [(dq.at[:, at], dq_mid.at[:, at], dq_out.at[:, at]) for at in steps]
    reads = [pltpu.make_async_copy(a, b, sems.at[0, i]) for i, (a, b, _) in enumerate(parts)]
    writes = [pltpu.make_async_copy(b, c, sems.at[1, i]) for i, (_, b, c) in enumerate(parts)]
    for copy in reads:
        copy.start()
    for read, write in zip(reads, writes):
        read.wait()
        write.start()
    for copy in writes:
        copy.wait()


def body(queries, out_grad, image_keys, image_values, link_ids, token_counts, tile_mask):
    smem = pl.BlockSpec(memory_space=pltpu.SMEM)
    vmem = pl.BlockSpec(memory_space=pltpu.VMEM)
    hbm = pl.BlockSpec(memory_space=pl.ANY)
    dma = pltpu.SemaphoreType.DMA
    lanes = 2 * TILE
    scratch = [
        pltpu.VMEM((TILE, H * HD), bf16),
        pltpu.VMEM((TILE, H * HD), bf16),
        pltpu.VMEM((TILE, H * HD), bf16),
        pltpu.VMEM((KVH, 2, NY, NZ, 2, ROWS, HD), bf16),
        pltpu.VMEM((BLOCKS, 2, ROWS, HD), bf16),
        pltpu.VMEM((LIVE, ROWS, 2 * HD), bf16),
        pltpu.VMEM((LIVE, ROWS, HD), bf16),
        pltpu.VMEM((KVH, HD, L), bf16),
        pltpu.VMEM((L, lanes), f32),
        pltpu.VMEM((L, lanes), f32),
        pltpu.VMEM((L, lanes), f32),
        pltpu.VMEM((L, lanes), f32),
        pltpu.VMEM((L, lanes), f32),
        pltpu.VMEM((L, lanes), bf16),
        pltpu.VMEM((L, lanes), bf16),
        pltpu.VMEM((KVH * PAIRS // 2, L, lanes), bf16),
        pltpu.VMEM((KVH * PAIRS // 2, L, lanes), bf16),
        pltpu.VMEM((LIVE + 1, ROWS, HD), f32),
        pltpu.VMEM((LIVE + 1, ROWS, HD), f32),
        pltpu.VMEM((KVH + 1, 2, NY, NZ, 2, ROWS, HD), bf16),
        pltpu.VMEM((KVH + 1, NY, NZ, 2, ROWS, HD), bf16),
        pltpu.VMEM((KVH + 1, NY, NZ, 2, ROWS, HD), bf16),
        pltpu.VMEM((KVH + 1, NY - 1, NZ, 2, ROWS, HD), bf16),
        pltpu.VMEM((KVH + 1, NZ, 2, ROWS, HD), bf16),
        pltpu.VMEM((KVH + 1, NZ - 1, 2, ROWS, HD), bf16),
        pltpu.VMEM((KVH + 1, 2, ROWS, HD), f32),
        pltpu.SMEM((LIVE,), jnp.int32),
        pltpu.SMEM((BLOCKS,), jnp.int32),
        pltpu.SMEM((LIVE,), jnp.int32),
        dma((2,)),
        dma((KVH,)),
        dma((NY,)),
        dma((NY,)),
        dma((KVH, NZ - 1)),
        dma((KVH, NZ - 1)),
        dma((KVH, NY - 1)),
        dma((KVH, NY - 1)),
        dma((KVH,)),
        dma((KVH,)),
        dma((KVH,)),
        dma((KVH,)),
        dma((KVH, NY - 1)),
        dma((KVH, NY - 1)),
        dma((KVH, NZ - 1)),
        dma((KVH, NZ - 1)),
    ]
    results = pl.pallas_call(
        kernel,
        out_shape=(
            jax.ShapeDtypeStruct((TILE, H * HD), bf16),
            jax.ShapeDtypeStruct((ROWS, KVH * HD), f32),
            jax.ShapeDtypeStruct((ROWS, KVH * HD), f32),
        ),
        in_specs=[smem, smem, smem, hbm, hbm, vmem, vmem],
        out_specs=[hbm, vmem, vmem],
        scratch_shapes=scratch,
        compiler_params=pltpu.CompilerParams(
            collective_id=0, has_side_effects=True, vmem_limit_bytes=56 << 20
        ),
        cost_estimate=pl.CostEstimate(
            flops=5 * 2 * TILE * H * L * HD, bytes_accessed=8 << 20, transcendentals=TILE * H * L
        ),
    )(link_ids, token_counts, tile_mask.T, queries, out_grad, image_keys, image_values)
    return pl.pallas_call(
        hand_out,
        out_shape=tuple(jax.ShapeDtypeStruct(r.shape, r.dtype) for r in results),
        in_specs=[hbm] * 3,
        out_specs=[hbm] * 3,
        scratch_shapes=[pltpu.VMEM(r.shape, r.dtype) for r in results] + [dma((2, HAND_STEPS + 2))],
    )(*results)


def solution(mesh):
    rows = P(("dp", "context"), None)
    return jax.shard_map(
        body,
        mesh=mesh,
        in_specs=(rows, rows, rows, rows, P("dp"), P("dp"), P("dp", None)),
        out_specs=(rows, rows, rows),
        check_vma=False,
    )
```
